32 devices in a mesh: seq: 8 (over y, x, core), fsdp: 4 (over z).
Axes of the slice: x: 2, y: 2, z: 4, core: 2. Of those that a mesh axis runs over, the one named last changes fastest.
Arguments:
- hidden: bfloat16 [4, 2048, 1024], P('fsdp', 'seq'), may hold values from -6 to 6
- in_weight: bfloat16 [1024, 4384], P('fsdp'), may hold values from -0.1875 to 0.1875
- conv_weight: bfloat16 [4, 2304], P(None, 'fsdp'), may hold values from -3 to 3
- conv_bias: bfloat16 [2304], P('fsdp'), may hold values from -3 to 3
- dt_bias: bfloat16 [32], P('fsdp'), may hold values from -6 to -3
- a_log: bfloat16 [32], P('fsdp'), may hold values from -4 to 2
- skip_gain: bfloat16 [32], P('fsdp'), may hold values from 0.5 to 1.5
- norm_gain: bfloat16 [1024], P('fsdp'), may hold values from 0.099609375 to 1.8984375
- gate_gain: bfloat16 [2048], P('fsdp'), may hold values from 0.099609375 to 1.8984375
- out_weight: bfloat16 [2048, 1024], P('fsdp'), may hold values from -0.125 to 0.125
- cotangent: bfloat16 [4, 2048, 1024], P('fsdp', 'seq'), may hold values from -6 to 6
Outputs:
- output: bfloat16 [4, 2048, 1024], P('fsdp', 'seq')
- hidden_grad: float32 [4, 2048, 1024], P('fsdp', 'seq')
- in_weight_grad: float32 [1024, 4384], P('fsdp')
- conv_weight_grad: float32 [4, 2304], P(None, 'fsdp')
- conv_bias_grad: float32 [2304], P('fsdp')
- dt_bias_grad: float32 [32], P('fsdp')
- a_log_grad: float32 [32], P('fsdp')
- skip_gain_grad: float32 [32], P('fsdp')
- norm_gain_grad: float32 [1024], P('fsdp')
- gate_gain_grad: float32 [2048], P('fsdp')
- out_weight_grad: float32 [2048, 1024], P('fsdp')
The draws below stay inside these ranges and needn't reach their ends.
All inputs are finite; a program needn't handle non-finite values.
Results may differ from the reference program's by a relative error of at most 0.0079.
Values may be sent and summed in bfloat16 or wider, within the bound.
A program may use at most 320 MiB of HBM per device.

```python
import jax
import jax.numpy as jnp
from jax import lax

D = 1024
H = 32
KCONV = 4
STRETCH = 256
E = 2048
CONVD = 2304
DPROJ = 4384
LENGTH = 2048
SEQS = 4


def block_scale(stream_key, dims, cuts, least, top_value):
    level, own = 1.0, jax.random.fold_in(stream_key, 6)
    for position, shards_of in cuts:
        draws = jnp.exp(jax.random.uniform(jax.random.fold_in(own, position), (shards_of,), jnp.float32, least / len(cuts), top_value / len(cuts)))
        level = level * jnp.repeat(draws, dims[position] // shards_of).reshape([-1 if axis == position else 1 for axis in range(len(dims))])
    return level


def scatter_about(key, dims, scale, limit, pieces=(), kind=jnp.bfloat16):
    loudness = block_scale(key, dims, pieces, -0.22, 0.18) if pieces else 1.0
    values = jax.random.normal(key, dims, jnp.float32) * scale * loudness
    return jnp.minimum(jnp.maximum(values, -limit), limit).astype(kind)


def setup_inputs(seed: int = 0) -> dict:
    arg_keys = jax.random.split(jax.random.key(seed), 12)
    hidden = scatter_about(arg_keys[0], (SEQS, LENGTH, D), 1.0, 6.0, ((0, 4), (1, 8)))
    in_weight = scatter_about(arg_keys[1], (D, DPROJ), D ** -0.5, 0.1875, ((0, 4),))
    conv_weight = scatter_about(arg_keys[2], (KCONV, CONVD), KCONV ** -0.5, 3.0, ((1, 4),))
    conv_bias = scatter_about(arg_keys[3], (CONVD,), 0.5, 3.0, ((0, 4),))
    dt_bias = jnp.clip(-6.0 + 3.0 * jax.random.uniform(arg_keys[4], (H,), jnp.float32) ** block_scale(arg_keys[4], (H,), ((0, 4),), -0.2, 0.2), -6.0, -3.0).astype(jnp.bfloat16)
    a_log = jnp.clip(-4.0 + 6.0 * jax.random.uniform(arg_keys[5], (H,), jnp.float32) ** block_scale(arg_keys[5], (H,), ((0, 4),), -0.2, 0.2), -4.0, 2.0).astype(jnp.bfloat16)
    skip_gain = jnp.clip(0.5 + 1.0 * jax.random.uniform(arg_keys[6], (H,), jnp.float32) ** block_scale(arg_keys[6], (H,), ((0, 4),), -0.2, 0.2), 0.5, 1.5).astype(jnp.bfloat16)
    norm_gain = jnp.clip(1.0 + 0.18 * jax.random.normal(arg_keys[7], (D,), jnp.float32), 0.099609375, 1.8984375).astype(jnp.bfloat16)
    gate_gain = jnp.clip(1.0 + 0.18 * jax.random.normal(arg_keys[8], (E,), jnp.float32), 0.099609375, 1.8984375).astype(jnp.bfloat16)
    out_weight = scatter_about(arg_keys[9], (E, D), E ** -0.5, 0.125, ((0, 4),))
    cotangent = scatter_about(arg_keys[10], (SEQS, LENGTH, D), 1.0, 6.0, ((0, 4), (1, 8)))
    return dict(hidden=hidden, in_weight=in_weight, conv_weight=conv_weight, conv_bias=conv_bias, dt_bias=dt_bias, a_log=a_log, skip_gain=skip_gain, norm_gain=norm_gain, gate_gain=gate_gain, out_weight=out_weight, cotangent=cotangent)


EPS = 1e-05
HIGH = lax.Precision.HIGHEST

@jax.custom_vjp
def low(v):
    return lax.optimization_barrier(v.astype(jnp.bfloat16)).astype(jnp.float32)

@jax.custom_vjp
def low_back(v):
    return v

def low_keep(v):
    return (low(v), None)

def low_pass(kept, grad):
    return (grad,)

def back_keep(v):
    return (v, None)

def back_low(kept, grad):
    return (low(grad),)
low.defvjp(low_keep, low_pass)
low_back.defvjp(back_keep, back_low)

def rms_scale(values):
    return lax.rsqrt(lax.optimization_barrier(jnp.mean(values * values, axis=-1, keepdims=True)) + EPS)

def causal_conv(values, weight, bias):
    kernel = weight.shape[0]
    length = values.shape[0]
    padded = jnp.pad(values, ((kernel - 1, 0), (0, 0)))
    total = jnp.broadcast_to(bias[None, :], values.shape)
    for step in range(kernel):
        total = total + weight[step][None, :] * padded[step:step + length]
    return jax.nn.silu(total)

def carry_states(states, ends):

    def advance(carry, item):
        block_state, block_end = item
        return (jnp.exp(block_end)[:, None, None] * carry + block_state, carry)
    begin = jnp.zeros(states.shape[1:], states.dtype)
    final, before = lax.scan(advance, begin, (states, ends))
    return before

def state_space(values, steps, rates, b_matrix, c_matrix):
    length, heads, head_size = values.shape
    blocks = length // STRETCH
    states_n = b_matrix.shape[1]
    x_blocks = values.reshape(blocks, STRETCH, heads, head_size)
    step_blocks = steps.reshape(blocks, STRETCH, heads)
    b_blocks = b_matrix.reshape(blocks, STRETCH, states_n)
    c_blocks = c_matrix.reshape(blocks, STRETCH, states_n)
    cumulative = jnp.cumsum(step_blocks * rates[None, None, :], axis=1)
    weighted = x_blocks * step_blocks[..., None]
    scores = jnp.einsum('cin,cjn->cij', c_blocks, b_blocks, precision=HIGH)
    row_index = lax.broadcasted_iota(jnp.int32, (STRETCH, STRETCH), 0)
    col_index = lax.broadcasted_iota(jnp.int32, (STRETCH, STRETCH), 1)
    lower = (row_index >= col_index)[None, :, :, None]
    spread = cumulative[:, :, None, :] - cumulative[:, None, :, :]
    decay = jnp.where(lower, jnp.exp(jnp.where(lower, spread, -60.0)), 0.0)
    within = jnp.einsum('cijh,cjhp->cihp', scores[..., None] * decay, weighted, precision=HIGH)
    ends = cumulative[:, -1, :]
    fading = jnp.exp(ends[:, None, :] - cumulative)
    states = jnp.einsum('cjn,cjhp->chnp', b_blocks, weighted * fading[..., None], precision=HIGH)
    before = carry_states(states, ends)
    carried = jnp.einsum('cin,chnp->cihp', c_blocks, before, precision=HIGH) * jnp.exp(cumulative)[..., None]
    return (within + carried).reshape(length, heads, head_size)

def mixer(x_heads, shared, raw_steps, conv_x, bias_x, conv_shared, bias_shared, step_bias, log_rates, skip_in):
    length = x_heads.shape[0]
    heads = raw_steps.shape[1]
    head_size = x_heads.shape[1] // heads
    half = shared.shape[1] // 2
    x_conv = causal_conv(x_heads, conv_x, bias_x)
    shared_conv = causal_conv(shared, conv_shared, bias_shared)
    steps = jax.nn.softplus(raw_steps + step_bias[None, :])
    rates = -jnp.exp(log_rates)
    values = x_conv.reshape(length, heads, head_size)
    result = state_space(values, steps, rates, shared_conv[:, :half], shared_conv[:, half:])
    result = result + skip_in[None, :, None] * values
    return result.reshape(length, heads * head_size)

def forward(hidden, in_weight, conv_weight, conv_bias, dt_bias, a_log, skip_gain, norm_gain, gate_gain, out_weight):
    inner = out_weight.shape[0]
    heads = a_log.shape[0]
    wide = in_weight.shape[1] - heads

    def sequence(units):
        normed = low(units * rms_scale(units) * norm_gain[None, :])
        projected = low_back(jnp.dot(normed, in_weight, precision=HIGH))
        gate = projected[:, :inner]
        x_part = low(projected[:, inner:2 * inner])
        shared = low(projected[:, 2 * inner:wide])
        raw_steps = low(projected[:, wide:])
        mixed = low_back(low(mixer(x_part, shared, raw_steps, conv_weight[:, :inner], conv_bias[:inner], conv_weight[:, inner:], conv_bias[inner:], dt_bias, a_log, skip_gain)))
        gated = mixed * jax.nn.silu(gate)
        scaled = low(gated * rms_scale(gated) * gate_gain[None, :])
        return units + jnp.dot(scaled, out_weight, precision=HIGH)
    return lax.map(jax.checkpoint(sequence), hidden)

def reference(hidden, in_weight, conv_weight, conv_bias, dt_bias, a_log, skip_gain, norm_gain, gate_gain, out_weight, cotangent):
    inputs = tuple((array.astype(jnp.float32) for array in (hidden, in_weight, conv_weight, conv_bias, dt_bias, a_log, skip_gain, norm_gain, gate_gain, out_weight)))
    output, pull = jax.vjp(forward, *inputs)
    grads = pull(cotangent.astype(jnp.float32))
    return (output.astype(jnp.bfloat16), grads[0], grads[1], grads[2], grads[3], grads[4], grads[5], grads[6], grads[7], grads[8], grads[9])
```

```python
import jax
import jax.numpy as jnp
from jax import lax
from jax.sharding import PartitionSpec as P

STRETCH = 256


EPS = 1e-05
HIGH = lax.Precision.HIGHEST
ROWS_RULE = (((0,), (0,)), ((), ()))
COLS_RULE = (((1,), (1,)), ((), ()))


def rms_scale(values):
    return lax.rsqrt(jnp.mean(values * values, axis=-1, keepdims=True) + EPS)


def causal_conv(values, weight, bias):
    kernel = weight.shape[0]
    length = values.shape[0]
    padded = jnp.pad(values, ((kernel - 1, 0), (0, 0)))
    total = jnp.broadcast_to(bias[None, :], values.shape)
    for step in range(kernel):
        total = total + weight[step][None, :] * padded[step : step + length]
    return jax.nn.silu(total)


def carry_states(states, ends):

    def advance(carry, item):
        block_state, block_end = item
        return (jnp.exp(block_end)[:, None, None] * carry + block_state, carry)

    begin = jnp.zeros(states.shape[1:], states.dtype)
    final, before = lax.scan(advance, begin, (states, ends))
    return before


def state_space(values, steps, rates, b_matrix, c_matrix):
    length, heads, head_size = values.shape
    blocks = length // STRETCH
    states_n = b_matrix.shape[1]
    x_blocks = values.reshape(blocks, STRETCH, heads, head_size)
    step_blocks = steps.reshape(blocks, STRETCH, heads)
    b_blocks = b_matrix.reshape(blocks, STRETCH, states_n)
    c_blocks = c_matrix.reshape(blocks, STRETCH, states_n)
    cumulative = jnp.cumsum(step_blocks * rates[None, None, :], axis=1)
    weighted = x_blocks * step_blocks[..., None]
    scores = jnp.einsum("cin,cjn->cij", c_blocks, b_blocks, precision=HIGH)
    row_index = lax.broadcasted_iota(jnp.int32, (STRETCH, STRETCH), 0)
    col_index = lax.broadcasted_iota(jnp.int32, (STRETCH, STRETCH), 1)
    lower = (row_index >= col_index)[None, :, :, None]
    spread = cumulative[:, :, None, :] - cumulative[:, None, :, :]
    decay = jnp.where(lower, jnp.exp(jnp.where(lower, spread, -60.0)), 0.0)
    within = jnp.einsum("cijh,cjhp->cihp", scores[..., None] * decay, weighted, precision=HIGH)
    ends = cumulative[:, -1, :]
    fading = jnp.exp(ends[:, None, :] - cumulative)
    states = jnp.einsum("cjn,cjhp->chnp", b_blocks, weighted * fading[..., None], precision=HIGH)
    before = carry_states(states, ends)
    carried = (
        jnp.einsum("cin,chnp->cihp", c_blocks, before, precision=HIGH)
        * jnp.exp(cumulative)[..., None]
    )
    return (within + carried).reshape(length, heads, head_size)


def mixer(
    x_heads,
    shared,
    raw_steps,
    conv_x,
    bias_x,
    conv_shared,
    bias_shared,
    step_bias,
    log_rates,
    skip_in,
):
    length = x_heads.shape[0]
    heads = raw_steps.shape[1]
    head_size = x_heads.shape[1] // heads
    half = shared.shape[1] // 2
    x_conv = causal_conv(x_heads, conv_x, bias_x)
    shared_conv = causal_conv(shared, conv_shared, bias_shared)
    steps = jax.nn.softplus(raw_steps + step_bias[None, :])
    rates = -jnp.exp(log_rates)
    values = x_conv.reshape(length, heads, head_size)
    result = state_space(values, steps, rates, shared_conv[:, :half], shared_conv[:, half:])
    result = result + skip_in[None, :, None] * values
    return result.reshape(length, heads * head_size)


def regrouped(
    hidden,
    in_weight,
    conv_weight,
    conv_bias,
    dt_bias,
    a_log,
    skip_gain,
    norm_gain,
    gate_gain,
    out_weight,
    cotangent,
):
    gathered = (
        lax.all_gather(in_weight, "fsdp", axis=0, tiled=True),
        lax.all_gather(conv_weight, "fsdp", axis=1, tiled=True),
        lax.all_gather(conv_bias, "fsdp", axis=0, tiled=True),
        lax.all_gather(dt_bias, "fsdp", axis=0, tiled=True),
        lax.all_gather(a_log, "fsdp", axis=0, tiled=True),
        lax.all_gather(skip_gain, "fsdp", axis=0, tiled=True),
        lax.all_gather(norm_gain, "fsdp", axis=0, tiled=True),
        lax.all_gather(gate_gain, "fsdp", axis=0, tiled=True),
        lax.all_gather(out_weight, "fsdp", axis=0, tiled=True),
    )
    w_in, w_conv, b_conv, bias_steps, log_rates, skip_full, gain_first, gain_second, w_out = (
        gathered
    )
    inner = w_out.shape[0]
    heads = log_rates.shape[0]
    wide = w_in.shape[1] - heads
    group = lax.axis_size("seq")
    per_group = heads // group
    head_size = inner // heads
    first = lax.axis_index("seq") * per_group
    units = hidden[0].astype(jnp.float32)
    scale_first = rms_scale(units)
    unit_normed = units * scale_first
    normed = (unit_normed * gain_first.astype(jnp.float32)[None, :]).astype(jnp.bfloat16)
    projected = jnp.dot(normed, w_in, preferred_element_type=jnp.float32)
    gate = projected[:, :inner]
    x_send = projected[:, inner : 2 * inner].astype(jnp.bfloat16)
    shared_send = projected[:, 2 * inner : wide].astype(jnp.bfloat16)
    steps_send = projected[:, wide:].astype(jnp.bfloat16)
    x_heads, step_heads = (
        lax.all_to_all(x_send, "seq", split_axis=1, concat_axis=0, tiled=True),
        lax.all_to_all(steps_send, "seq", split_axis=1, concat_axis=0, tiled=True),
    )
    shared_all = lax.all_gather(shared_send, "seq", axis=0, tiled=True)

    def local_mix(x_in, shared_in, steps_in, conv_full, bias_full, step_bias, rates_log, skip_in):
        conv_x = lax.dynamic_slice_in_dim(conv_full, first * head_size, per_group * head_size, 1)
        bias_x = lax.dynamic_slice_in_dim(bias_full, first * head_size, per_group * head_size, 0)
        own_bias = lax.dynamic_slice_in_dim(step_bias, first, per_group, 0)
        own_rates = lax.dynamic_slice_in_dim(rates_log, first, per_group, 0)
        own_skip = lax.dynamic_slice_in_dim(skip_in, first, per_group, 0)
        return mixer(
            x_in,
            shared_in,
            steps_in,
            conv_x,
            bias_x,
            conv_full[:, inner:],
            bias_full[inner:],
            own_bias,
            own_rates,
            own_skip,
        )

    mixed, pull = jax.vjp(
        local_mix,
        x_heads.astype(jnp.float32),
        shared_all.astype(jnp.float32),
        step_heads.astype(jnp.float32),
        w_conv.astype(jnp.float32),
        b_conv.astype(jnp.float32),
        bias_steps.astype(jnp.float32),
        log_rates.astype(jnp.float32),
        skip_full.astype(jnp.float32),
    )
    mixed_tokens = lax.all_to_all(
        mixed.astype(jnp.bfloat16), "seq", split_axis=0, concat_axis=1, tiled=True
    ).astype(jnp.float32)
    gate_act = jax.nn.silu(gate)
    gated = mixed_tokens * gate_act
    scale_second = rms_scale(gated)
    unit_gated = gated * scale_second
    scaled = (unit_gated * gain_second.astype(jnp.float32)[None, :]).astype(jnp.bfloat16)
    output = (units + jnp.dot(scaled, w_out, preferred_element_type=jnp.float32)).astype(
        jnp.bfloat16
    )
    back_in, again_first, again_second, back_out = (
        lax.all_gather(in_weight, "fsdp", axis=0, tiled=True),
        lax.all_gather(norm_gain, "fsdp", axis=0, tiled=True),
        lax.all_gather(gate_gain, "fsdp", axis=0, tiled=True),
        lax.all_gather(out_weight, "fsdp", axis=0, tiled=True),
    )
    upstream = cotangent[0]
    grad_out_w = lax.dot_general(scaled, upstream, ROWS_RULE, preferred_element_type=jnp.float32)
    grad_scaled = lax.dot_general(upstream, back_out, COLS_RULE, preferred_element_type=jnp.float32)
    grad_gate_gain = jnp.sum(grad_scaled * unit_gated, axis=0)
    grad_unit = grad_scaled * again_second.astype(jnp.float32)[None, :]
    grad_gated = scale_second * (
        grad_unit - unit_gated * jnp.mean(grad_unit * unit_gated, axis=-1, keepdims=True)
    )
    grad_mixed = (grad_gated * gate_act).astype(jnp.bfloat16)
    sigma = jax.nn.sigmoid(gate)
    grad_gate = grad_gated * mixed_tokens * sigma * (1.0 + gate * (1.0 - sigma))
    grad_heads = lax.all_to_all(grad_mixed, "seq", split_axis=1, concat_axis=0, tiled=True)
    (
        grad_x,
        grad_shared,
        grad_steps,
        grad_conv,
        grad_conv_bias,
        grad_step_bias,
        grad_rates,
        grad_skip,
    ) = pull(grad_heads.astype(jnp.float32))
    back_x, back_steps = (
        lax.all_to_all(grad_x.astype(jnp.bfloat16), "seq", split_axis=0, concat_axis=1, tiled=True),
        lax.all_to_all(
            grad_steps.astype(jnp.bfloat16), "seq", split_axis=0, concat_axis=1, tiled=True
        ),
    )
    shared_tokens = lax.psum_scatter(
        grad_shared.astype(jnp.bfloat16), "seq", scatter_dimension=0, tiled=True
    ).astype(jnp.float32)
    grad_projected = jnp.concatenate(
        [grad_gate, back_x.astype(jnp.float32), shared_tokens, back_steps.astype(jnp.float32)],
        axis=1,
    ).astype(jnp.bfloat16)
    grad_in_w = lax.dot_general(
        normed, grad_projected, ROWS_RULE, preferred_element_type=jnp.float32
    )
    grad_normed = lax.dot_general(
        grad_projected, back_in, COLS_RULE, preferred_element_type=jnp.float32
    )
    grad_norm_gain = jnp.sum(grad_normed * unit_normed, axis=0)
    grad_first = grad_normed * again_first.astype(jnp.float32)[None, :]
    grad_units = upstream.astype(jnp.float32) + scale_first * (
        grad_first - unit_normed * jnp.mean(grad_first * unit_normed, axis=-1, keepdims=True)
    )
    shard_grads = (
        lax.psum_scatter(grad_in_w, "fsdp", scatter_dimension=0, tiled=True),
        lax.psum_scatter(grad_conv, "fsdp", scatter_dimension=1, tiled=True),
        lax.psum_scatter(grad_conv_bias, "fsdp", scatter_dimension=0, tiled=True),
        lax.psum_scatter(grad_step_bias, "fsdp", scatter_dimension=0, tiled=True),
        lax.psum_scatter(grad_rates, "fsdp", scatter_dimension=0, tiled=True),
        lax.psum_scatter(grad_skip, "fsdp", scatter_dimension=0, tiled=True),
        lax.psum_scatter(grad_norm_gain, "fsdp", scatter_dimension=0, tiled=True),
        lax.psum_scatter(grad_gate_gain, "fsdp", scatter_dimension=0, tiled=True),
        lax.psum_scatter(grad_out_w, "fsdp", scatter_dimension=0, tiled=True),
    )
    totals = lax.psum(
        (
            shard_grads[0],
            shard_grads[1],
            shard_grads[2],
            shard_grads[3],
            shard_grads[4],
            shard_grads[5],
            shard_grads[6],
            shard_grads[7],
            shard_grads[8],
        ),
        "seq",
    )
    return (
        output[None],
        grad_units[None],
        totals[0],
        totals[1],
        totals[2],
        totals[3],
        totals[4],
        totals[5],
        totals[6],
        totals[7],
        totals[8],
    )


def per_device(
    hidden,
    in_weight,
    conv_weight,
    conv_bias,
    dt_bias,
    a_log,
    skip_gain,
    norm_gain,
    gate_gain,
    out_weight,
    cotangent,
):
    shards = lax.axis_size("fsdp")
    group = lax.axis_size("seq")
    shard_heads = a_log.shape[0]
    if shard_heads % group:
        return regrouped(
            hidden,
            in_weight,
            conv_weight,
            conv_bias,
            dt_bias,
            a_log,
            skip_gain,
            norm_gain,
            gate_gain,
            out_weight,
            cotangent,
        )
    f32, bf16 = jnp.float32, jnp.bfloat16
    place = lax.axis_index("seq")
    column = lax.axis_index("fsdp")
    part = shard_heads // group
    heads = shard_heads * shards
    inner = out_weight.shape[0] * shards
    size = inner // heads
    own = shards * part
    chans = own * size
    rows_in = in_weight.shape[0]
    wide = in_weight.shape[1] - heads
    shared_n = wide - 2 * inner
    taps = conv_weight.shape[0]
    convd = conv_weight.shape[1] * shards
    width = hidden.shape[2]
    tokens = hidden.shape[1]

    def pick(full, unit):
        view = full.reshape(full.shape[:-1] + (shards, group, part * unit))
        mine = lax.dynamic_index_in_dim(view, place, full.ndim, keepdims=False)
        return mine.reshape(full.shape[:-1] + (own * unit,))

    def spread(mine, unit):
        view = mine.reshape(mine.shape[:-1] + (shards, 1, part * unit))
        full = jnp.zeros(mine.shape[:-1] + (shards, group, part * unit), mine.dtype)
        full = lax.dynamic_update_slice_in_dim(full, view, place, mine.ndim)
        return full.reshape(mine.shape[:-1] + (heads * unit,))

    def shard_of(full):
        count = full.shape[-1] // shards
        return lax.dynamic_slice_in_dim(full, column * count, count, full.ndim - 1)

    hidden_all = lax.all_gather(hidden[0], "seq", axis=0, tiled=True)
    small = jnp.concatenate(
        [
            conv_weight.reshape(-1),
            conv_bias,
            dt_bias,
            a_log,
            skip_gain,
            norm_gain,
            gate_gain,
        ]
    )
    small_all = lax.all_gather(small, "fsdp", axis=0, tiled=False).astype(f32)
    in_own = jnp.concatenate(
        [
            pick(in_weight[:, :inner], size),
            pick(in_weight[:, inner : 2 * inner], size),
            in_weight[:, 2 * inner : wide],
            pick(in_weight[:, wide:], 1),
        ],
        axis=1,
    )
    w_in = lax.all_gather(in_own, "fsdp", axis=0, tiled=True)
    out_own = lax.dynamic_slice_in_dim(out_weight, place * part * size, part * size, 0)
    w_out = lax.all_gather(out_own, "fsdp", axis=0, tiled=True)
    upstream = lax.all_gather(cotangent[0], "seq", axis=0, tiled=True)

    at = 0
    pieces = []
    for count in (taps * convd, convd, heads, heads, heads, width, inner):
        count = count // shards
        pieces.append(small_all[:, at : at + count])
        at += count
    w_conv = pieces[0].reshape(shards, taps, convd // shards)
    w_conv = jnp.transpose(w_conv, (1, 0, 2)).reshape(taps, convd)
    b_conv, bias_steps, log_rates, skip_full, gain_first, gain_second = (
        piece.reshape(-1) for piece in pieces[1:]
    )
    gain_own = pick(gain_second, size)[None, :]

    units = hidden_all.astype(f32)
    unit_normed = units * rms_scale(units)
    normed = (unit_normed * gain_first[None, :]).astype(bf16)
    projected = jnp.dot(normed, w_in, preferred_element_type=f32)
    gate = projected[:, :chans]
    x_raw = projected[:, chans : 2 * chans].astype(bf16)
    shared_raw = projected[:, 2 * chans : 2 * chans + shared_n].astype(bf16)
    steps_raw = projected[:, 2 * chans + shared_n :].astype(bf16)

    grad_scaled = lax.dot_general(upstream, w_out, COLS_RULE, preferred_element_type=f32)

    mixed, pull = jax.vjp(
        mixer,
        x_raw.astype(f32),
        shared_raw.astype(f32),
        steps_raw.astype(f32),
        pick(w_conv[:, :inner], size),
        pick(b_conv[:inner], size),
        w_conv[:, inner:],
        b_conv[inner:],
        pick(bias_steps, 1),
        pick(log_rates, 1),
        pick(skip_full, 1),
    )
    mixed = mixed.astype(bf16).astype(f32)
    sigma = jax.nn.sigmoid(gate)
    gate_act = gate * sigma
    gated = mixed * gate_act
    grad_unit = grad_scaled * gain_own
    sums = lax.psum(
        jnp.stack([jnp.sum(gated * gated, axis=1), jnp.sum(grad_unit * gated, axis=1)]), "seq"
    )
    scale_second = lax.rsqrt(sums[0] / inner + EPS)[:, None]
    average = scale_second * sums[1][:, None] / inner
    unit_gated = gated * scale_second
    scaled = (unit_gated * gain_own).astype(bf16)
    partial_out = jnp.dot(scaled, w_out, preferred_element_type=f32).astype(bf16)
    output = lax.psum_scatter(partial_out, "seq", scatter_dimension=0, tiled=True)
    output = (hidden[0].astype(f32) + output.astype(f32)).astype(bf16)

    grad_out_w = lax.dot_general(scaled, upstream, ROWS_RULE, preferred_element_type=f32)
    grad_out_w = lax.psum_scatter(
        grad_out_w.astype(bf16), "fsdp", scatter_dimension=0, tiled=True
    )
    grad_out_w = lax.all_gather(grad_out_w, "seq", axis=0, tiled=True).astype(f32)

    grad_gate_gain = jnp.sum(grad_scaled * unit_gated, axis=0)
    grad_gated = scale_second * (grad_unit - unit_gated * average)
    grad_mixed = (grad_gated * gate_act).astype(bf16)
    grad_gate = (grad_gated * mixed * sigma * (1.0 + gate * (1.0 - sigma))).astype(bf16)
    (
        grad_x,
        grad_shared,
        grad_steps,
        grad_conv_x,
        grad_bias_x,
        grad_conv_shared,
        grad_bias_shared,
        grad_step_bias,
        grad_rates,
        grad_skip,
    ) = pull(grad_mixed.astype(f32))
    grad_projected = jnp.concatenate(
        [grad_gate, grad_x.astype(bf16), grad_shared.astype(bf16), grad_steps.astype(bf16)], axis=1
    )
    grad_normed = lax.dot_general(grad_projected, w_in, COLS_RULE, preferred_element_type=f32)
    grad_norm_gain = jnp.sum(grad_normed * unit_normed, axis=0)
    grad_tokens = lax.psum_scatter(
        grad_normed.astype(bf16), "seq", scatter_dimension=0, tiled=True
    ).astype(f32)
    grad_in_w = lax.dot_general(normed, grad_projected, ROWS_RULE, preferred_element_type=f32)
    grad_in_w = lax.psum_scatter(grad_in_w.astype(bf16), "fsdp", scatter_dimension=0, tiled=True)
    grad_in_w = lax.all_gather(grad_in_w, "seq", axis=0, tiled=False).astype(f32)

    def settle(piece, unit):
        view = piece.reshape(group, rows_in, shards, part * unit)
        return jnp.transpose(view, (1, 2, 0, 3)).reshape(rows_in, heads * unit)

    grad_in_w = jnp.concatenate(
        [
            settle(grad_in_w[:, :, :chans], size),
            settle(grad_in_w[:, :, chans : 2 * chans], size),
            jnp.sum(grad_in_w[:, :, 2 * chans : 2 * chans + shared_n], axis=0),
            settle(grad_in_w[:, :, 2 * chans + shared_n :], 1),
        ],
        axis=1,
    )

    tokens_f = hidden[0].astype(f32)
    scale_first = rms_scale(tokens_f)
    own_normed = tokens_f * scale_first
    grad_first = grad_tokens * gain_first[None, :]
    grad_units = cotangent[0].astype(f32) + scale_first * (
        grad_first - own_normed * jnp.mean(grad_first * own_normed, axis=-1, keepdims=True)
    )

    small_grads = lax.psum(
        jnp.concatenate(
            [
                jnp.concatenate([spread(grad_conv_x, size), grad_conv_shared], axis=1).reshape(-1),
                spread(grad_bias_x, size),
                grad_bias_shared,
                spread(grad_step_bias, 1),
                spread(grad_rates, 1),
                spread(grad_skip, 1),
                grad_norm_gain,
                spread(grad_gate_gain, size),
            ]
        ),
        ("seq", "fsdp"),
    )
    at = 0
    totals = []
    for count in (taps * convd, convd, heads, heads, heads, width, inner):
        piece = small_grads[at : at + count]
        at += count
        if count == taps * convd:
            piece = piece.reshape(taps, convd)
        totals.append(shard_of(piece))
    return (output[None], grad_units[None], grad_in_w, *totals, grad_out_w)


def solution(mesh):
    in_specs = (
        P("fsdp", "seq", None),
        P("fsdp", None),
        P(None, "fsdp"),
        P("fsdp"),
        P("fsdp"),
        P("fsdp"),
        P("fsdp"),
        P("fsdp"),
        P("fsdp"),
        P("fsdp", None),
        P("fsdp", "seq", None),
    )
    out_specs = (
        P("fsdp", "seq", None),
        P("fsdp", "seq", None),
        P("fsdp", None),
        P(None, "fsdp"),
        P("fsdp"),
        P("fsdp"),
        P("fsdp"),
        P("fsdp"),
        P("fsdp"),
        P("fsdp"),
        P("fsdp", None),
    )
    return jax.shard_map(
        per_device, mesh=mesh, in_specs=in_specs, out_specs=out_specs, check_vma=False
    )
```

```python
import functools

import jax
import jax.numpy as jnp
from jax import lax
from jax.experimental import pallas as pl
from jax.experimental.pallas import tpu as pltpu
from jax.sharding import PartitionSpec as P

STRETCH = 256


EPS = 1e-05
HIGH = lax.Precision.HIGHEST
ROWS_RULE = (((0,), (0,)), ((), ()))
COLS_RULE = (((1,), (1,)), ((), ()))


def rms_scale(values):
    return lax.rsqrt(jnp.mean(values * values, axis=-1, keepdims=True) + EPS)


def causal_conv(values, weight, bias):
    kernel = weight.shape[0]
    length = values.shape[0]
    padded = jnp.pad(values, ((kernel - 1, 0), (0, 0)))
    total = jnp.broadcast_to(bias[None, :], values.shape)
    for step in range(kernel):
        total = total + weight[step][None, :] * padded[step : step + length]
    return jax.nn.silu(total)


def carry_states(states, ends):

    def advance(carry, item):
        block_state, block_end = item
        return (jnp.exp(block_end)[:, None, None] * carry + block_state, carry)

    begin = jnp.zeros(states.shape[1:], states.dtype)
    final, before = lax.scan(advance, begin, (states, ends))
    return before


def state_space(values, steps, rates, b_matrix, c_matrix):
    length, heads, head_size = values.shape
    blocks = length // STRETCH
    states_n = b_matrix.shape[1]
    x_blocks = values.reshape(blocks, STRETCH, heads, head_size)
    step_blocks = steps.reshape(blocks, STRETCH, heads)
    b_blocks = b_matrix.reshape(blocks, STRETCH, states_n)
    c_blocks = c_matrix.reshape(blocks, STRETCH, states_n)
    cumulative = jnp.cumsum(step_blocks * rates[None, None, :], axis=1)
    weighted = x_blocks * step_blocks[..., None]
    scores = jnp.einsum("cin,cjn->cij", c_blocks, b_blocks, precision=HIGH)
    row_index = lax.broadcasted_iota(jnp.int32, (STRETCH, STRETCH), 0)
    col_index = lax.broadcasted_iota(jnp.int32, (STRETCH, STRETCH), 1)
    lower = (row_index >= col_index)[None, :, :, None]
    spread = cumulative[:, :, None, :] - cumulative[:, None, :, :]
    decay = jnp.where(lower, jnp.exp(jnp.where(lower, spread, -60.0)), 0.0)
    within = jnp.einsum("cijh,cjhp->cihp", scores[..., None] * decay, weighted, precision=HIGH)
    ends = cumulative[:, -1, :]
    fading = jnp.exp(ends[:, None, :] - cumulative)
    states = jnp.einsum("cjn,cjhp->chnp", b_blocks, weighted * fading[..., None], precision=HIGH)
    before = carry_states(states, ends)
    carried = (
        jnp.einsum("cin,chnp->cihp", c_blocks, before, precision=HIGH)
        * jnp.exp(cumulative)[..., None]
    )
    return (within + carried).reshape(length, heads, head_size)


def mixer(
    x_heads,
    shared,
    raw_steps,
    conv_x,
    bias_x,
    conv_shared,
    bias_shared,
    step_bias,
    log_rates,
    skip_in,
):
    length = x_heads.shape[0]
    heads = raw_steps.shape[1]
    head_size = x_heads.shape[1] // heads
    half = shared.shape[1] // 2
    x_conv = causal_conv(x_heads, conv_x, bias_x)
    shared_conv = causal_conv(shared, conv_shared, bias_shared)
    steps = jax.nn.softplus(raw_steps + step_bias[None, :])
    rates = -jnp.exp(log_rates)
    values = x_conv.reshape(length, heads, head_size)
    result = state_space(values, steps, rates, shared_conv[:, :half], shared_conv[:, half:])
    result = result + skip_in[None, :, None] * values
    return result.reshape(length, heads * head_size)


F32, BF16 = jnp.float32, jnp.bfloat16
LANES = 128


def tile_dot(left, right, rule=(((1,), (0,)), ((), ()))):
    return lax.dot_general(
        left.astype(BF16), right.astype(BF16), rule, preferred_element_type=F32
    )


def sharp_dot(left, right, rule=(((1,), (0,)), ((), ()))):
    left_top, right_top = left.astype(BF16), right.astype(BF16)
    left_low = (left - left_top.astype(F32)).astype(BF16)
    right_low = (right - right_top.astype(F32)).astype(BF16)
    return (
        tile_dot(left_top, right_top, rule)
        + tile_dot(left_low, right_top, rule)
        + tile_dot(left_top, right_low, rule)
    )


def full_dot(left, right, rule=(((1,), (0,)), ((), ()))):
    return lax.dot_general(left, right, rule, precision=HIGH, preferred_element_type=F32)


def block_values(first, chans, own, size, now_ref, tail_ref, conv_ref, head_ref):
    rows = now_ref.shape[0]
    conv_n = conv_ref.shape[1]
    half = (conv_n - chans) // 2
    raw = now_ref[:, chans : chans + conv_n].astype(BF16).astype(F32)
    tail = tail_ref[:, chans : chans + conv_n].astype(BF16).astype(F32)
    tail = jnp.where(first, 0.0, tail)
    ext = jnp.concatenate([tail, raw], axis=0)
    pre = conv_ref[4:5, :]
    taps = []
    for k in range(4):
        taps.append(ext[5 + k : 5 + k + rows])
        pre = pre + conv_ref[k : k + 1, :] * taps[k]
    sig = 1.0 / (1.0 + jnp.exp(-pre))
    act = pre * sig
    x = act[:, :chans]
    b = act[:, chans : chans + half]
    c = act[:, chans + half :]
    step = now_ref[:, chans + conv_n : chans + conv_n + LANES].astype(BF16).astype(F32)
    lane = lax.broadcasted_iota(jnp.int32, (rows, LANES), 1)
    step = jnp.where(lane < own, step, 0.0) + head_ref[0:1, :]
    dt = jnp.maximum(step, 0.0) + jnp.log1p(jnp.exp(-jnp.abs(step)))
    low = lax.broadcasted_iota(jnp.int32, (rows, rows), 0) >= lax.broadcasted_iota(
        jnp.int32, (rows, rows), 1
    )
    tri = jnp.where(low, 1.0, 0.0)
    cum = full_dot(tri, dt * head_ref[1:2, :])
    cum_rows = jnp.transpose(cum)
    end = cum[rows - 1 : rows, :]
    widen = jnp.where(
        lax.broadcasted_iota(jnp.int32, (LANES, chans), 1) // size
        == lax.broadcasted_iota(jnp.int32, (LANES, chans), 0),
        1.0,
        0.0,
    )
    decays = [
        jnp.exp(jnp.where(low, cum[:, h : h + 1] - cum_rows[h : h + 1, :], -jnp.inf))
        for h in range(own)
    ]
    scores = sharp_dot(c, b, COLS_RULE)
    wide = full_dot(jnp.concatenate([dt, jnp.exp(cum), jnp.exp(end - cum)], axis=0), widen)
    dt_w, grow_w, fade_w = wide[:rows], wide[rows : 2 * rows], wide[2 * rows :]
    owner = lax.broadcasted_iota(jnp.int32, (rows, chans), 1) // size
    return dict(
        pre=pre, sig=sig, taps=taps, x=x, b=b, c=c, step=step, dt=dt, tri=tri, end=end,
        widen=widen, decays=decays, scores=scores, dt_w=dt_w, grow_w=grow_w, fade_w=fade_w,
        owner=owner, conv_n=conv_n, half=half, rows=rows,
    )


def scan_forward(own, size, now_ref, tail_ref, conv_ref, head_ref, chan_ref, mixed_ref, before_ref, carry):
    chans = own * size
    first = pl.program_id(0) == 0

    @pl.when(first)
    def _():
        carry[...] = jnp.zeros_like(carry)

    v = block_values(first, chans, own, size, now_ref, tail_ref, conv_ref, head_ref)
    weighted = v["x"] * v["dt_w"]
    before = carry[...]
    before_ref[0] = before
    total = sharp_dot(v["c"], before) * v["grow_w"] + chan_ref[0:1, :] * v["x"]
    for h in range(own):
        part = jnp.where(v["owner"] == h, weighted, 0.0)
        total = total + sharp_dot(v["scores"] * v["decays"][h], part)
    mixed_ref[...] = total.astype(BF16)
    state = sharp_dot(v["b"], weighted * v["fade_w"], ROWS_RULE)
    carry[...] = v["grow_w"][v["rows"] - 1 :, :] * before + state


def scan_backward(
    own, size, inner, now_ref, tail_ref, conv_ref, head_ref, chan_ref, mixed_ref, scaled_ref, row_ref,
    before_ref, grad_ref, conv_out, head_out, chan_out, carry, ahead,
):
    chans = own * size
    turn = pl.program_id(0)
    first = turn == pl.num_programs(0) - 1

    @pl.when(turn == 0)
    def _():
        carry[...] = jnp.zeros_like(carry)
        ahead[...] = jnp.zeros_like(ahead)
        conv_out[...] = jnp.zeros_like(conv_out)
        head_out[...] = jnp.zeros_like(head_out)
        chan_out[...] = jnp.zeros_like(chan_out)

    v = block_values(first, chans, own, size, now_ref, tail_ref, conv_ref, head_ref)
    rows, conv_n, half = v["rows"], v["conv_n"], v["half"]
    gate = now_ref[:, :chans]
    mixed = mixed_ref[...].astype(F32)
    sigma = 1.0 / (1.0 + jnp.exp(-gate))
    gate_act = gate * sigma
    scale, average = row_ref[:, 0:1], row_ref[:, 1:2]
    unit = mixed * gate_act * scale
    back = scaled_ref[...]
    chan_out[1:2, :] += jnp.sum(back * unit, axis=0, keepdims=True)
    grad_gated = scale * (back * chan_ref[1:2, :] - unit * average)
    dy = (grad_gated * gate_act).astype(BF16).astype(F32)
    grad_ref[:, :chans] = (grad_gated * mixed * sigma * (1.0 + gate * (1.0 - sigma))).astype(BF16)

    x, b, c = v["x"], v["b"], v["c"]
    chan_out[0:1, :] += jnp.sum(dy * x, axis=0, keepdims=True)
    weighted = x * v["dt_w"]
    before = before_ref[0]
    grad_next = carry[...]
    end_w = v["grow_w"][rows - 1 :, :]

    grad_scores = jnp.zeros((rows, rows), F32)
    grad_weighted = jnp.zeros((rows, chans), F32)
    lane = lax.broadcasted_iota(jnp.int32, (rows, LANES), 1)
    row_sums = jnp.zeros((rows, LANES), F32)
    col_sums = []
    for h in range(own):
        dy_h = jnp.where(v["owner"] == h, dy, 0.0)
        grad_decayed = tile_dot(dy_h, weighted, COLS_RULE)
        spread = grad_decayed * v["decays"][h]
        grad_scores = grad_scores + spread
        moved = spread * v["scores"]
        row_sums = jnp.where(lane == h, jnp.sum(moved, axis=1, keepdims=True), row_sums)
        col_sums.append(jnp.sum(moved, axis=0, keepdims=True))
        grad_weighted = grad_weighted + sharp_dot(
            v["scores"] * v["decays"][h], dy_h, ROWS_RULE
        )
    col_sums = jnp.concatenate(col_sums + [jnp.zeros((LANES - own, rows), F32)], axis=0)

    outer = sharp_dot(c, before)
    dz = dy * v["grow_w"]
    faded = weighted * v["fade_w"]
    grad_faded = sharp_dot(b, grad_next)
    grad_c = tile_dot(grad_scores, b) + tile_dot(dz, before, COLS_RULE)
    grad_b = tile_dot(grad_scores, c, ROWS_RULE) + tile_dot(faded, grad_next, COLS_RULE)
    grad_weighted = grad_weighted + grad_faded * v["fade_w"]
    left = jnp.concatenate([dz * outer, grad_faded * faded, grad_weighted * x], axis=0)
    sums = full_dot(left, v["widen"], COLS_RULE)
    from_outer, from_fade, grad_dt = sums[:rows], sums[rows : 2 * rows], sums[2 * rows :]
    kept = jnp.sum(grad_next * before, axis=0, keepdims=True) * end_w
    kept = full_dot(jnp.broadcast_to(kept, (8, chans)), v["widen"], COLS_RULE)[0:1]
    grad_end = kept + jnp.sum(from_fade, axis=0, keepdims=True)
    carry[...] = end_w * grad_next + sharp_dot(c, dz, ROWS_RULE)

    grad_cum = row_sums - jnp.transpose(col_sums) + from_outer - from_fade
    grad_rate = full_dot(v["tri"], grad_cum, ROWS_RULE) + grad_end
    rate = head_ref[1:2, :]
    grad_dt = grad_dt + rate * grad_rate
    grad_step = grad_dt / (1.0 + jnp.exp(-v["step"]))
    grad_step = jnp.where(lane < own, grad_step, 0.0)
    head_out[0:1, :] += jnp.sum(grad_step, axis=0, keepdims=True)
    head_out[1:2, :] += jnp.sum(grad_rate * v["dt"], axis=0, keepdims=True) * rate
    grad_ref[:, chans + conv_n :] = grad_step.astype(BF16)

    grad_x = chan_ref[0:1, :] * dy + grad_weighted * v["dt_w"]
    grad_act = jnp.concatenate([grad_x, grad_b, grad_c], axis=1)
    grad_pre = grad_act * v["sig"] * (1.0 + v["pre"] * (1.0 - v["sig"]))
    conv_out[4:5, :] += jnp.sum(grad_pre, axis=0, keepdims=True)
    ext = jnp.concatenate([grad_pre, ahead[...]], axis=0)
    grad_in = jnp.zeros((rows, conv_n), F32)
    for k in range(4):
        conv_out[k : k + 1, :] += jnp.sum(grad_pre * v["taps"][k], axis=0, keepdims=True)
        grad_in = grad_in + conv_ref[k : k + 1, :] * ext[3 - k : 3 - k + rows]
    ahead[...] = grad_pre[0:8]
    grad_ref[:, chans : chans + conv_n] = grad_in.astype(BF16)


def run_forward(projected, conv, head, chan, own, size):
    length, columns = projected.shape
    chans = own * size
    conv_n = conv.shape[1]
    states = (conv_n - chans) // 2
    blocks = length // STRETCH
    per = STRETCH // 8
    fixed = lambda i: (0, 0)
    return pl.pallas_call(
        functools.partial(scan_forward, own, size),
        grid=(blocks,),
        in_specs=[
            pl.BlockSpec((STRETCH, columns), lambda i: (i, 0)),
            pl.BlockSpec((8, columns), lambda i: (jnp.maximum(i * per - 1, 0), 0)),
            pl.BlockSpec(conv.shape, fixed),
            pl.BlockSpec(head.shape, fixed),
            pl.BlockSpec(chan.shape, fixed),
        ],
        out_specs=[
            pl.BlockSpec((STRETCH, chans), lambda i: (i, 0)),
            pl.BlockSpec((1, states, chans), lambda i: (i, 0, 0)),
        ],
        out_shape=[
            jax.ShapeDtypeStruct((length, chans), BF16),
            jax.ShapeDtypeStruct((blocks, states, chans), F32),
        ],
        scratch_shapes=[pltpu.VMEM((states, chans), F32)],
        compiler_params=pltpu.CompilerParams(vmem_limit_bytes=40 * 2**20),
        cost_estimate=pl.CostEstimate(
            flops=blocks * 400_000_000, bytes_accessed=length * columns * 6, transcendentals=0
        ),
    )(projected, projected, conv, head, chan)


def run_backward(projected, conv, head, chan, mixed, grad_scaled, row_stats, before, own, size, inner):
    length, columns = projected.shape
    chans = own * size
    conv_n = conv.shape[1]
    states = (conv_n - chans) // 2
    blocks = length // STRETCH
    per = STRETCH // 8
    fixed = lambda i: (0, 0)
    last = blocks - 1
    return pl.pallas_call(
        functools.partial(scan_backward, own, size, inner),
        grid=(blocks,),
        in_specs=[
            pl.BlockSpec((STRETCH, columns), lambda i: (last - i, 0)),
            pl.BlockSpec((8, columns), lambda i: (jnp.maximum((last - i) * per - 1, 0), 0)),
            pl.BlockSpec(conv.shape, fixed),
            pl.BlockSpec(head.shape, fixed),
            pl.BlockSpec(chan.shape, fixed),
            pl.BlockSpec((STRETCH, chans), lambda i: (last - i, 0)),
            pl.BlockSpec((STRETCH, chans), lambda i: (last - i, 0)),
            pl.BlockSpec((STRETCH, row_stats.shape[1]), lambda i: (last - i, 0)),
            pl.BlockSpec((1, states, chans), lambda i: (last - i, 0, 0)),
        ],
        out_specs=[
            pl.BlockSpec((STRETCH, columns), lambda i: (last - i, 0)),
            pl.BlockSpec((8, conv_n), fixed),
            pl.BlockSpec((8, LANES), fixed),
            pl.BlockSpec((8, chans), fixed),
        ],
        out_shape=[
            jax.ShapeDtypeStruct((length, columns), BF16),
            jax.ShapeDtypeStruct((8, conv_n), F32),
            jax.ShapeDtypeStruct((8, LANES), F32),
            jax.ShapeDtypeStruct((8, chans), F32),
        ],
        scratch_shapes=[pltpu.VMEM((states, chans), F32), pltpu.VMEM((8, conv_n), F32)],
        compiler_params=pltpu.CompilerParams(vmem_limit_bytes=48 * 2**20),
        cost_estimate=pl.CostEstimate(
            flops=blocks * 800_000_000, bytes_accessed=length * columns * 12, transcendentals=0
        ),
    )(projected, projected, conv, head, chan, mixed, grad_scaled, row_stats, before)


def regrouped(
    hidden,
    in_weight,
    conv_weight,
    conv_bias,
    dt_bias,
    a_log,
    skip_gain,
    norm_gain,
    gate_gain,
    out_weight,
    cotangent,
):
    gathered = (
        lax.all_gather(in_weight, "fsdp", axis=0, tiled=True),
        lax.all_gather(conv_weight, "fsdp", axis=1, tiled=True),
        lax.all_gather(conv_bias, "fsdp", axis=0, tiled=True),
        lax.all_gather(dt_bias, "fsdp", axis=0, tiled=True),
        lax.all_gather(a_log, "fsdp", axis=0, tiled=True),
        lax.all_gather(skip_gain, "fsdp", axis=0, tiled=True),
        lax.all_gather(norm_gain, "fsdp", axis=0, tiled=True),
        lax.all_gather(gate_gain, "fsdp", axis=0, tiled=True),
        lax.all_gather(out_weight, "fsdp", axis=0, tiled=True),
    )
    w_in, w_conv, b_conv, bias_steps, log_rates, skip_full, gain_first, gain_second, w_out = (
        gathered
    )
    inner = w_out.shape[0]
    heads = log_rates.shape[0]
    wide = w_in.shape[1] - heads
    group = lax.axis_size("seq")
    per_group = heads // group
    head_size = inner // heads
    first = lax.axis_index("seq") * per_group
    units = hidden[0].astype(jnp.float32)
    scale_first = rms_scale(units)
    unit_normed = units * scale_first
    normed = (unit_normed * gain_first.astype(jnp.float32)[None, :]).astype(jnp.bfloat16)
    projected = jnp.dot(normed, w_in, preferred_element_type=jnp.float32)
    gate = projected[:, :inner]
    x_send = projected[:, inner : 2 * inner].astype(jnp.bfloat16)
    shared_send = projected[:, 2 * inner : wide].astype(jnp.bfloat16)
    steps_send = projected[:, wide:].astype(jnp.bfloat16)
    x_heads, step_heads = (
        lax.all_to_all(x_send, "seq", split_axis=1, concat_axis=0, tiled=True),
        lax.all_to_all(steps_send, "seq", split_axis=1, concat_axis=0, tiled=True),
    )
    shared_all = lax.all_gather(shared_send, "seq", axis=0, tiled=True)

    def local_mix(x_in, shared_in, steps_in, conv_full, bias_full, step_bias, rates_log, skip_in):
        conv_x = lax.dynamic_slice_in_dim(conv_full, first * head_size, per_group * head_size, 1)
        bias_x = lax.dynamic_slice_in_dim(bias_full, first * head_size, per_group * head_size, 0)
        own_bias = lax.dynamic_slice_in_dim(step_bias, first, per_group, 0)
        own_rates = lax.dynamic_slice_in_dim(rates_log, first, per_group, 0)
        own_skip = lax.dynamic_slice_in_dim(skip_in, first, per_group, 0)
        return mixer(
            x_in,
            shared_in,
            steps_in,
            conv_x,
            bias_x,
            conv_full[:, inner:],
            bias_full[inner:],
            own_bias,
            own_rates,
            own_skip,
        )

    mixed, pull = jax.vjp(
        local_mix,
        x_heads.astype(jnp.float32),
        shared_all.astype(jnp.float32),
        step_heads.astype(jnp.float32),
        w_conv.astype(jnp.float32),
        b_conv.astype(jnp.float32),
        bias_steps.astype(jnp.float32),
        log_rates.astype(jnp.float32),
        skip_full.astype(jnp.float32),
    )
    mixed_tokens = lax.all_to_all(
        mixed.astype(jnp.bfloat16), "seq", split_axis=0, concat_axis=1, tiled=True
    ).astype(jnp.float32)
    gate_act = jax.nn.silu(gate)
    gated = mixed_tokens * gate_act
    scale_second = rms_scale(gated)
    unit_gated = gated * scale_second
    scaled = (unit_gated * gain_second.astype(jnp.float32)[None, :]).astype(jnp.bfloat16)
    output = (units + jnp.dot(scaled, w_out, preferred_element_type=jnp.float32)).astype(
        jnp.bfloat16
    )
    back_in, again_first, again_second, back_out = (
        lax.all_gather(in_weight, "fsdp", axis=0, tiled=True),
        lax.all_gather(norm_gain, "fsdp", axis=0, tiled=True),
        lax.all_gather(gate_gain, "fsdp", axis=0, tiled=True),
        lax.all_gather(out_weight, "fsdp", axis=0, tiled=True),
    )
    upstream = cotangent[0]
    grad_out_w = lax.dot_general(scaled, upstream, ROWS_RULE, preferred_element_type=jnp.float32)
    grad_scaled = lax.dot_general(upstream, back_out, COLS_RULE, preferred_element_type=jnp.float32)
    grad_gate_gain = jnp.sum(grad_scaled * unit_gated, axis=0)
    grad_unit = grad_scaled * again_second.astype(jnp.float32)[None, :]
    grad_gated = scale_second * (
        grad_unit - unit_gated * jnp.mean(grad_unit * unit_gated, axis=-1, keepdims=True)
    )
    grad_mixed = (grad_gated * gate_act).astype(jnp.bfloat16)
    sigma = jax.nn.sigmoid(gate)
    grad_gate = grad_gated * mixed_tokens * sigma * (1.0 + gate * (1.0 - sigma))
    grad_heads = lax.all_to_all(grad_mixed, "seq", split_axis=1, concat_axis=0, tiled=True)
    (
        grad_x,
        grad_shared,
        grad_steps,
        grad_conv,
        grad_conv_bias,
        grad_step_bias,
        grad_rates,
        grad_skip,
    ) = pull(grad_heads.astype(jnp.float32))
    back_x, back_steps = (
        lax.all_to_all(grad_x.astype(jnp.bfloat16), "seq", split_axis=0, concat_axis=1, tiled=True),
        lax.all_to_all(
            grad_steps.astype(jnp.bfloat16), "seq", split_axis=0, concat_axis=1, tiled=True
        ),
    )
    shared_tokens = lax.psum_scatter(
        grad_shared.astype(jnp.bfloat16), "seq", scatter_dimension=0, tiled=True
    ).astype(jnp.float32)
    grad_projected = jnp.concatenate(
        [grad_gate, back_x.astype(jnp.float32), shared_tokens, back_steps.astype(jnp.float32)],
        axis=1,
    ).astype(jnp.bfloat16)
    grad_in_w = lax.dot_general(
        normed, grad_projected, ROWS_RULE, preferred_element_type=jnp.float32
    )
    grad_normed = lax.dot_general(
        grad_projected, back_in, COLS_RULE, preferred_element_type=jnp.float32
    )
    grad_norm_gain = jnp.sum(grad_normed * unit_normed, axis=0)
    grad_first = grad_normed * again_first.astype(jnp.float32)[None, :]
    grad_units = upstream.astype(jnp.float32) + scale_first * (
        grad_first - unit_normed * jnp.mean(grad_first * unit_normed, axis=-1, keepdims=True)
    )
    shard_grads = (
        lax.psum_scatter(grad_in_w, "fsdp", scatter_dimension=0, tiled=True),
        lax.psum_scatter(grad_conv, "fsdp", scatter_dimension=1, tiled=True),
        lax.psum_scatter(grad_conv_bias, "fsdp", scatter_dimension=0, tiled=True),
        lax.psum_scatter(grad_step_bias, "fsdp", scatter_dimension=0, tiled=True),
        lax.psum_scatter(grad_rates, "fsdp", scatter_dimension=0, tiled=True),
        lax.psum_scatter(grad_skip, "fsdp", scatter_dimension=0, tiled=True),
        lax.psum_scatter(grad_norm_gain, "fsdp", scatter_dimension=0, tiled=True),
        lax.psum_scatter(grad_gate_gain, "fsdp", scatter_dimension=0, tiled=True),
        lax.psum_scatter(grad_out_w, "fsdp", scatter_dimension=0, tiled=True),
    )
    totals = lax.psum(
        (
            shard_grads[0],
            shard_grads[1],
            shard_grads[2],
            shard_grads[3],
            shard_grads[4],
            shard_grads[5],
            shard_grads[6],
            shard_grads[7],
            shard_grads[8],
        ),
        "seq",
    )
    return (
        output[None],
        grad_units[None],
        totals[0],
        totals[1],
        totals[2],
        totals[3],
        totals[4],
        totals[5],
        totals[6],
        totals[7],
        totals[8],
    )


def per_device(
    hidden,
    in_weight,
    conv_weight,
    conv_bias,
    dt_bias,
    a_log,
    skip_gain,
    norm_gain,
    gate_gain,
    out_weight,
    cotangent,
):
    shards = lax.axis_size("fsdp")
    group = lax.axis_size("seq")
    shard_heads = a_log.shape[0]
    if shard_heads % group:
        return regrouped(
            hidden,
            in_weight,
            conv_weight,
            conv_bias,
            dt_bias,
            a_log,
            skip_gain,
            norm_gain,
            gate_gain,
            out_weight,
            cotangent,
        )
    f32, bf16 = jnp.float32, jnp.bfloat16
    place = lax.axis_index("seq")
    part = shard_heads // group
    heads = shard_heads * shards
    inner = out_weight.shape[0] * shards
    size = inner // heads
    own = shards * part
    chans = own * size
    rows_in = in_weight.shape[0]
    wide = in_weight.shape[1] - heads
    shared_n = wide - 2 * inner
    taps = conv_weight.shape[0]
    convd = conv_weight.shape[1] * shards
    width = hidden.shape[2]

    def pick(full, unit):
        view = full.reshape(full.shape[:-1] + (shards, group, part * unit))
        mine = lax.dynamic_index_in_dim(view, place, full.ndim, keepdims=False)
        return mine.reshape(full.shape[:-1] + (own * unit,))

    def spread(mine, unit):
        view = mine.reshape(mine.shape[:-1] + (shards, 1, part * unit))
        full = jnp.zeros(mine.shape[:-1] + (shards, group, part * unit), mine.dtype)
        full = lax.dynamic_update_slice_in_dim(full, view, place, mine.ndim)
        return full.reshape(mine.shape[:-1] + (heads * unit,))

    small = jnp.concatenate(
        [
            conv_weight.reshape(-1),
            conv_bias,
            dt_bias,
            a_log,
            skip_gain,
            norm_gain,
            gate_gain,
        ]
    )
    small_n = small.shape[0]
    spare = LANES // 2
    held = -(-small_n // spare)
    step_pad = spare - own
    in_own = jnp.concatenate(
        [
            pick(in_weight[:, :inner], size),
            pick(in_weight[:, inner : 2 * inner], size),
            in_weight[:, 2 * inner : wide],
            jnp.pad(pick(in_weight[:, wide:], 1), ((0, 0), (0, step_pad))),
            jnp.pad(
                jnp.pad(small, (0, held * spare - small_n)).reshape(held, spare),
                ((0, rows_in - held), (0, 0)),
            ),
        ],
        axis=1,
    )
    columns = in_own.shape[1]
    w_in = lax.all_gather(in_own, "fsdp", axis=0, tiled=True)
    hidden_all = lax.all_gather(hidden[0], "seq", axis=0, tiled=True)
    out_own = lax.dynamic_slice_in_dim(out_weight, place * part * size, part * size, 0)
    w_out = lax.all_gather(out_own, "fsdp", axis=0, tiled=True)
    later, hidden_all = lax.optimization_barrier((cotangent[0], hidden_all))
    upstream = lax.all_gather(later, "seq", axis=0, tiled=True)

    small_all = w_in[:, columns - spare :].reshape(shards, rows_in * spare).astype(f32)
    at = 0
    pieces = []
    for count in (taps * convd, convd, heads, heads, heads, width, inner):
        count = count // shards
        pieces.append(small_all[:, at : at + count])
        at += count
    w_conv = pieces[0].reshape(shards, taps, convd // shards)
    w_conv = jnp.transpose(w_conv, (1, 0, 2)).reshape(taps, convd)
    b_conv, bias_steps, log_rates, skip_full, gain_first, gain_second = (
        piece.reshape(-1) for piece in pieces[1:]
    )
    gain_own = pick(gain_second, size)[None, :]
    conv_rows = jnp.concatenate([w_conv, b_conv[None, :]], axis=0)
    conv_own = jnp.concatenate([pick(conv_rows[:, :inner], size), conv_rows[:, inner:]], axis=1)
    conv_own = jnp.pad(conv_own, ((0, 3), (0, 0)))
    head_own = jnp.stack([pick(bias_steps, 1), -jnp.exp(pick(log_rates, 1))])
    head_own = jnp.pad(head_own, ((0, 6), (0, LANES - own)))
    chan_own = jnp.stack([jnp.repeat(pick(skip_full, 1), size), gain_own[0]])
    chan_own = jnp.pad(chan_own, ((0, 6), (0, 0)))

    units = hidden_all.astype(f32)
    unit_normed = units * rms_scale(units)
    normed = (unit_normed * gain_first[None, :]).astype(bf16)
    projected = jnp.dot(normed, w_in, preferred_element_type=f32)
    gate = projected[:, :chans]
    mixed_low, before = run_forward(projected, conv_own, head_own, chan_own, own, size)
    grad_scaled = lax.dot_general(upstream, w_out, COLS_RULE, preferred_element_type=f32)

    gated = mixed_low.astype(f32) * jax.nn.silu(gate)
    sums = lax.psum(
        jnp.stack(
            [jnp.sum(gated * gated, axis=1), jnp.sum(grad_scaled * gain_own * gated, axis=1)]
        ),
        "seq",
    )
    scale_second = lax.rsqrt(sums[0] / inner + EPS)
    average = scale_second * sums[1] / inner
    row_stats = jnp.stack([scale_second, average], axis=1)
    scaled = (gated * scale_second[:, None] * gain_own).astype(bf16)
    partial_out = jnp.dot(scaled, w_out, preferred_element_type=f32).astype(bf16)
    output = lax.psum_scatter(partial_out, "seq", scatter_dimension=0, tiled=True)
    output = (hidden[0].astype(f32) + output.astype(f32)).astype(bf16)

    grad_out_w = lax.dot_general(scaled, upstream, ROWS_RULE, preferred_element_type=f32)
    grad_out_w = lax.psum_scatter(
        grad_out_w.astype(bf16), "fsdp", scatter_dimension=0, tiled=True
    )
    grad_out_w = lax.all_gather(grad_out_w, "seq", axis=0, tiled=True).astype(f32)

    grad_projected, conv_grads, head_grads, chan_grads = run_backward(
        projected, conv_own, head_own, chan_own, mixed_low, grad_scaled, row_stats, before,
        own, size, inner,
    )
    grad_in_w = lax.dot_general(normed, grad_projected, ROWS_RULE, preferred_element_type=f32)
    grad_normed = lax.dot_general(
        grad_projected[:, : columns - LANES + own],
        w_in[:, : columns - LANES + own],
        COLS_RULE,
        preferred_element_type=f32,
    )
    grad_norm_gain = jnp.sum(grad_normed * unit_normed, axis=0)

    conv_full = jnp.concatenate([spread(conv_grads[:5, :chans], size), conv_grads[:5, chans:]], axis=1)
    by_shard = lambda full: full.reshape(shards, -1)
    skip_grads = jnp.sum(chan_grads[0].reshape(own, size), axis=1)
    conv_taps = jnp.transpose(conv_full[:taps].reshape(taps, shards, convd // shards), (1, 0, 2))
    small_grads = jnp.concatenate(
        [
            conv_taps.reshape(shards, -1),
            by_shard(conv_full[4]),
            by_shard(spread(head_grads[0, :own], 1)),
            by_shard(spread(head_grads[1, :own], 1)),
            by_shard(spread(skip_grads, 1)),
            by_shard(grad_norm_gain),
            by_shard(spread(chan_grads[1], size)),
        ],
        axis=1,
    )
    small_grads = jnp.pad(small_grads, ((0, 0), (0, held * spare - small_n)))
    small_grads = jnp.pad(
        small_grads.reshape(shards, held, spare), ((0, 0), (0, rows_in - held), (0, 0))
    ).reshape(width, spare)
    grad_in_w = jnp.concatenate([grad_in_w[:, : columns - spare], small_grads], axis=1)
    grad_in_w = lax.psum_scatter(grad_in_w.astype(bf16), "fsdp", scatter_dimension=0, tiled=True)
    grad_in_w = lax.all_gather(grad_in_w, "seq", axis=0, tiled=False).astype(f32)
    grad_tokens = lax.psum_scatter(
        grad_normed.astype(bf16), "seq", scatter_dimension=0, tiled=True
    ).astype(f32)

    def settle(piece, unit):
        view = piece.reshape(group, rows_in, shards, part * unit)
        return jnp.transpose(view, (1, 2, 0, 3)).reshape(rows_in, heads * unit)

    small_sum = jnp.sum(grad_in_w[:, :held, columns - spare :], axis=0).reshape(-1)
    at = 2 * chans
    grad_in_full = jnp.concatenate(
        [
            settle(grad_in_w[:, :, :chans], size),
            settle(grad_in_w[:, :, chans:at], size),
            jnp.sum(grad_in_w[:, :, at : at + shared_n], axis=0),
            settle(grad_in_w[:, :, at + shared_n : at + shared_n + own], 1),
        ],
        axis=1,
    )

    tokens_f = hidden[0].astype(f32)
    scale_first = rms_scale(tokens_f)
    own_normed = tokens_f * scale_first
    grad_first = grad_tokens * gain_first[None, :]
    grad_units = cotangent[0].astype(f32) + scale_first * (
        grad_first - own_normed * jnp.mean(grad_first * own_normed, axis=-1, keepdims=True)
    )

    at = 0
    totals = []
    for count in (taps * convd, convd, heads, heads, heads, width, inner):
        piece = small_sum[at : at + count // shards]
        at += count // shards
        if count == taps * convd:
            piece = piece.reshape(taps, convd // shards)
        totals.append(piece)
    return (output[None], grad_units[None], grad_in_full, *totals, grad_out_w)


def solution(mesh):
    in_specs = (
        P("fsdp", "seq", None),
        P("fsdp", None),
        P(None, "fsdp"),
        P("fsdp"),
        P("fsdp"),
        P("fsdp"),
        P("fsdp"),
        P("fsdp"),
        P("fsdp"),
        P("fsdp", None),
        P("fsdp", "seq", None),
    )
    out_specs = (
        P("fsdp", "seq", None),
        P("fsdp", "seq", None),
        P("fsdp", None),
        P(None, "fsdp"),
        P("fsdp"),
        P("fsdp"),
        P("fsdp"),
        P("fsdp"),
        P("fsdp"),
        P("fsdp"),
        P("fsdp", None),
    )
    return jax.shard_map(
        per_device, mesh=mesh, in_specs=in_specs, out_specs=out_specs, check_vma=False
    )
```
